512 devices in a mesh: row: 32 (over y_hi, z, core), col: 16 (over x, y_lo).
Axes of the slice: x: 4, y: 8 (y_hi: 2, y_lo: 4; y = y_hi * 4 + y_lo), z: 8, core: 2. Of those that a mesh axis runs over, the one named last changes fastest.
Arguments:
- inputs: bfloat16 [2048, 12288], P('col', 'row'), may hold values from -0.29882812 to 0.29882812
- preact: bfloat16 [2048, 24576], P('row', 'col'), may hold values from -8 to 8
- out_grad: bfloat16 [2048, 24576], P('row', 'col'), may hold values from -6 to 6
- weight: bfloat16 [12288, 24576], P('row', 'col'), may hold values from -0.0546875 to 0.0546875
Outputs:
- input_grad: bfloat16 [2048, 12288], P('col', 'row')
- weight_grad: float32 [12288, 24576], P('row', 'col')
The draws below stay inside these ranges and needn't reach their ends.
All inputs are finite; a program needn't handle non-finite values.
Results may differ from the reference program's by a relative error of at most 0.0049.
Values may be sent and summed in bfloat16 or wider, within the bound.
A program may use at most 64 MiB of HBM per device.

```python
import math
import jax
import jax.numpy as jnp
from jax import lax

D = 12288
FF = 24576
TOKENS = 2048


def level_of(stream_key, dims, cuts, smallest, high):
    factor_of = 1.0
    for axis_at, parts in cuts:
        draws = jax.random.uniform(jax.random.fold_in(jax.random.fold_in(stream_key, 6), axis_at), (parts,), jnp.float32, smallest / len(cuts), high / len(cuts))
        factor_of = factor_of * jnp.repeat(jnp.exp(draws), dims[axis_at] // parts).reshape((-1,) + (1,) * (len(dims) - 1 - axis_at))
    return factor_of


def centred(own_key, shape, deviation, limit, shards=(), dtype=jnp.bfloat16):
    entries = jax.random.normal(own_key, shape, jnp.float32) * deviation
    if len(shards) > 0:
        entries = level_of(own_key, shape, shards, -0.22, 0.18) * entries
    return jnp.clip(entries, min=-limit, max=limit).astype(dtype)


def setup_inputs(seed: int = 0) -> dict:
    streams_of = jax.random.split(jax.random.key(seed), 5)
    return {
        "inputs": centred(streams_of[0], (TOKENS, D), 0.05, 0.29882812, ((0, 16), (1, 32))),
        "preact": centred(streams_of[1], (TOKENS, FF), 1.5, 8.0, ((0, 32), (1, 16))),
        "out_grad": centred(streams_of[2], (TOKENS, FF), 1.0, 6.0, ((0, 32), (1, 16))),
        "weight": centred(streams_of[3], (D, FF), D ** -0.5, 0.0546875, ((0, 32), (1, 16))),
    }


def gelu_slope(preact_f):
    coeff = math.sqrt(2.0 / math.pi)
    inner = coeff * (preact_f + 0.044715 * preact_f * preact_f * preact_f)
    tanh_val = jnp.tanh(inner)
    return 0.5 * (1.0 + tanh_val) + 0.5 * preact_f * (1.0 - tanh_val * tanh_val) * coeff * (1.0 + 3.0 * 0.044715 * preact_f * preact_f)

def reference(inputs, preact, out_grad, weight):
    hidden_grad = (out_grad.astype(jnp.float32) * gelu_slope(preact.astype(jnp.float32))).astype(jnp.bfloat16)
    input_grad = lax.dot_general(hidden_grad, weight, (((1,), (1,)), ((), ())), preferred_element_type=jnp.float32).astype(jnp.bfloat16)
    weight_grad = lax.dot_general(inputs, hidden_grad, (((0,), (0,)), ((), ())), preferred_element_type=jnp.float32)
    return (input_grad, weight_grad)
```

```python
import functools
import math

import jax
import jax.numpy as jnp
from jax import lax
from jax.experimental import pallas as pl
from jax.experimental.pallas import tpu as pltpu
from jax.sharding import PartitionSpec as P

MESH = pl.DeviceIdType.MESH
F32, BF16 = jnp.float32, jnp.bfloat16

NX, NYL, NYH, NZ = 4, 4, 2, 8
ROWS, HID, WID = 64, 1536, 384
CHUNK = ROWS // 2
TOK = 2 * ROWS
TOKENS = TOK * NYH * NZ
RIGHT, LEFT = 0, 1


def gelu_slope(preact_f):
    coeff = math.sqrt(2.0 / math.pi)
    inner = coeff * (preact_f + 0.044715 * preact_f * preact_f * preact_f)
    tanh_val = jnp.tanh(inner)
    return 0.5 * (1.0 + tanh_val) + 0.5 * preact_f * (1.0 - tanh_val * tanh_val) * coeff * (
        1.0 + 3.0 * 0.044715 * preact_f * preact_f
    )


def kernel(
    x_ref, pre_ref, grad_ref, w_hbm, ig_ref, wg_hbm,
    h, xs, w, xt, wg, g_own, g_out, g_in, s_out, s_in, g_fin,
    w_sem, wg_sem,
    hy_send, hy_recv, hz_send, hz_recv, hc_send, hc_recv,
    xy_send, xy_recv, xx_send, xx_recv,
    gx_send, gx_recv, gy_send, gy_recv,
):
    r, c = lax.axis_index("row"), lax.axis_index("col")
    yh, z, core = r // (2 * NZ), (r // 2) % NZ, r % 2
    x, yl = c // NYL, c % NYL

    def dev(yh_=yh, z_=z, core_=core, x_=x, yl_=yl):
        return ((yh_ * NZ + z_) * 2 + core_, x_ * NYL + yl_)

    def copy(src, dst, ssem, rsem, to):
        return pltpu.make_async_remote_copy(
            src_ref=src, dst_ref=dst, send_sem=ssem, recv_sem=rsem, device_id=to, device_id_type=MESH
        )

    w_copy = pltpu.make_async_copy(w_hbm, w, w_sem)
    w_copy.start()

    partner = dev(yh_=1 - yh)
    sibling = dev(core_=1 - core)
    ahead, behind = dev(z_=(z + 1) % NZ), dev(z_=(z + NZ - 1) % NZ)
    peers = [partner, sibling, ahead, behind]
    peers += [dev(x_=(x + d) % NX) for d in range(1, NX)]
    peers += [dev(yl_=(yl + d) % NYL) for d in range(1, NYL)]
    barrier = pltpu.get_barrier_semaphore()
    for peer in peers:
        pl.semaphore_signal(barrier, inc=1, device_id=peer, device_id_type=MESH)

    def rows(yh_, z_, core_, chunk=None):
        base = ((yh_ * NZ + z_) * 2 + core_) * ROWS
        if chunk is None:
            return pl.ds(pl.multiple_of(base, ROWS), ROWS)
        return pl.ds(pl.multiple_of(base + chunk * CHUNK, CHUNK), CHUNK)

    def side(s):
        return yh if s == 0 else 1 - yh

    def make_hidden(chunk):
        at = pl.ds(chunk * CHUNK, CHUNK)
        h[rows(yh, z, core, chunk), :] = (
            grad_ref[at, :].astype(F32) * gelu_slope(pre_ref[at, :].astype(F32))
        ).astype(BF16)

    def ring(s, k, way, chunk, z_from):
        block = h.at[rows(side(s), z_from, core, chunk)]
        return copy(
            block, block, hz_send.at[s, way, k, chunk], hz_recv.at[s, way, k, chunk],
            ahead if way == RIGHT else behind,
        )

    def across(chunk, yh_):
        block = h.at[rows(yh_, z, core, chunk)]
        return copy(block, block, hy_send.at[chunk], hy_recv.at[chunk], partner)

    def share(s, slot, z_from, core_):
        block = h.at[rows(side(s), z_from, core_)]
        return copy(block, block, hc_send.at[s, slot], hc_recv.at[s, slot], sibling)

    def origin(way, k):
        return (z + NZ - k) % NZ if way == RIGHT else (z + k) % NZ

    def x_block(x_, yl_):
        return xs.at[pl.ds(pl.multiple_of((x_ * NYL + yl_) * TOK, TOK), TOK)]

    def x_near(d, to_or_from):
        return copy(
            x_ref, x_block(x, to_or_from), xy_send.at[d - 1], xy_recv.at[d - 1], dev(yl_=(yl + d) % NYL)
        )

    def x_far(d, x_):
        block = xs.at[pl.ds(pl.multiple_of(x_ * NYL * TOK, NYL * TOK), NYL * TOK)]
        return copy(block, block, xx_send.at[d - 1], xx_recv.at[d - 1], dev(x_=(x + d) % NX))

    make_hidden(0)
    pl.semaphore_wait(barrier, len(peers))
    for chunk in (0, 1):
        if chunk:
            make_hidden(1)
        across(chunk, yh).start()
        ring(0, 1, RIGHT, chunk, z).start()
        ring(0, 1, LEFT, chunk, z).start()
    share(0, 0, z, core).start()
    for d in range(1, NYL):
        x_near(d, yl).start()
    x_block(x, yl)[...] = x_ref[...]
    w_copy.wait()

    def home(s, z_from):
        return side(s) * (NZ // NYL) + z_from // NYL, z_from % NYL

    def part_out(s, z_from, x_to, j):
        d = (x + NX - x_to) % NX
        at = side(s) * NZ + z_from
        return copy(
            g_out.at[at], g_in.at[d - 1, j], gx_send.at[at], gx_recv.at[d - 1, j], dev(x_=x_to)
        )

    def product(s, slot, z_from):
        share(s, slot, z_from, 1 - core).wait_recv()
        at = pl.ds(pl.multiple_of((side(s) * NZ + z_from) * TOK, TOK), TOK)
        part = lax.dot_general(h[at, :], w[...], (((1,), (1,)), ((), ())), preferred_element_type=F32)
        x_to, j = home(s, z_from)

        @pl.when(x_to == x)
        def _():
            g_own[j] = part

        @pl.when(x_to != x)
        def _():
            g_out[side(s) * NZ + z_from] = part.astype(BF16)
            part_out(s, z_from, x_to, j).start()

    def sum_out(j):
        d = (yl + NYL - j) % NYL
        return copy(s_out.at[j], s_in.at[d - 1], gy_send.at[j], gy_recv.at[d - 1], dev(yl_=j))

    def reduce_x(s, z_from):
        x_to, j = home(s, z_from)

        @pl.when(x_to == x)
        def _():
            total = g_own[j]
            for d in range(1, NX):
                copy(g_out.at[0], g_in.at[d - 1, j], gx_send.at[0], gx_recv.at[d - 1, j], sibling).wait_recv()
                total = total + g_in[d - 1, j].astype(F32)

            @pl.when(j == yl)
            def _():
                g_fin[...] = total

            @pl.when(j != yl)
            def _():
                s_out[j] = total.astype(BF16)
                sum_out(j).start()

    def pass_on(s, k, way, chunk):
        z_from = origin(way, k)
        ring(s, k, way, chunk, z_from).wait_recv()

        @pl.when((k < 3) | (chunk == way))
        def _():
            ring(s, k + 1, way, chunk, z_from).start()

    def forward(s, k):
        for chunk in (0, 1):
            pass_on(s, k, RIGHT, chunk)
            pass_on(s, k, LEFT, chunk)
        share(s, k, origin(RIGHT, k), core).start()
        share(s, 3 + k, origin(LEFT, k), core).start()

    def last(s):
        far = origin(RIGHT, 4)
        ring(s, 4, RIGHT, 0, far).wait_recv()
        ring(s, 4, LEFT, 1, far).wait_recv()
        share(s, 7, far, core).start()

    product(0, 0, z)

    @pl.loop(1, 4)
    def _(k):
        forward(0, k)

        @pl.when(k == 2)
        def _():
            for d in range(1, NYL):
                x_near(d, (yl + NYL - d) % NYL).wait_recv()
            for d in range(1, NX):
                x_far(d, x).start()

        product(0, k, origin(RIGHT, k))
        product(0, 3 + k, origin(LEFT, k))

    for chunk in (0, 1):
        across(chunk, 1 - yh).wait_recv()
        ring(1, 1, RIGHT, chunk, z).start()
        ring(1, 1, LEFT, chunk, z).start()
    share(1, 0, z, core).start()
    last(0)
    product(1, 0, z)
    product(0, 7, origin(RIGHT, 4))
    reduce_x(0, z)

    @pl.loop(1, 4)
    def _(k):
        forward(1, k)
        product(1, k, origin(RIGHT, k))
        product(1, 3 + k, origin(LEFT, k))
        reduce_x(0, origin(RIGHT, k))
        reduce_x(0, origin(LEFT, k))

        @pl.when(k == 1)
        def _():
            reduce_x(0, origin(RIGHT, 4))
            reduce_x(1, z)

        @pl.when(k > 1)
        def _():
            reduce_x(1, origin(RIGHT, k - 1))
            reduce_x(1, origin(LEFT, k - 1))

    last(1)
    product(1, 7, origin(RIGHT, 4))

    for d in range(1, NX):
        x_far(d, (x + NX - d) % NX).wait_recv()
    half = TOKENS // 2
    piece = 384
    n_pieces = HID // piece

    def transpose(yh_):
        at = pl.multiple_of(yh_ * half, half)
        for i in range(half // 256):
            xt[:, pl.ds(i * 256, 256)] = xs[pl.ds(at + i * 256, 256), :].T

    def outer(yh_, n):
        at = pl.ds(pl.multiple_of(yh_ * half, half), half)
        cols = pl.ds(pl.multiple_of(n * piece, piece), piece)
        return cols, jnp.dot(xt[...], h[at, cols], preferred_element_type=F32)

    transpose(yh)

    @pl.loop(0, n_pieces)
    def _(n):
        cols, value = outer(yh, n)
        wg[:, cols] = value

    reduce_x(1, origin(RIGHT, 3))
    reduce_x(1, origin(LEFT, 3))
    reduce_x(1, origin(RIGHT, 4))
    transpose(1 - yh)

    def wg_copy(n):
        cols = pl.ds(pl.multiple_of(n * piece, piece), piece)
        return pltpu.make_async_copy(wg.at[:, cols], wg_hbm.at[:, cols], wg_sem.at[n])

    @pl.loop(0, n_pieces)
    def _(n):
        cols, value = outer(1 - yh, n)
        wg[:, cols] += value
        wg_copy(n).start()

    total = g_fin[...]
    for d in range(1, NYL):
        copy(s_out.at[0], s_in.at[d - 1], gy_send.at[0], gy_recv.at[d - 1], sibling).wait_recv()
        total = total + s_in[d - 1].astype(F32)
    ig_ref[...] = total.astype(BF16)

    for n in range(n_pieces):
        wg_copy(n).wait()
    for chunk in (0, 1):
        across(chunk, yh).wait_send()
    for s in (0, 1):
        for way in (RIGHT, LEFT):
            for k in range(1, 5):
                for chunk in (0, 1):
                    if k < 4 or chunk == way:
                        ring(s, k, way, chunk, z).wait_send()
        for slot in range(8):
            share(s, slot, z, core).wait_send()
    for d in range(1, NYL):
        x_near(d, yl).wait_send()
    for d in range(1, NX):
        x_far(d, x).wait_send()

    @pl.loop(0, NYH * NZ)
    def _(at):
        @pl.when(at // NYL != x)
        def _():
            copy(g_out.at[at], g_in.at[0, 0], gx_send.at[at], gx_recv.at[0, 0], sibling).wait_send()

    @pl.loop(0, NYL)
    def _(j):
        @pl.when(j != yl)
        def _():
            copy(s_out.at[j], s_in.at[0], gy_send.at[j], gy_recv.at[0], sibling).wait_send()


def shards(inputs, preact, out_grad, weight):
    vmem = pl.BlockSpec(memory_space=pltpu.VMEM)
    hbm = pl.BlockSpec(memory_space=pl.ANY)
    dma = pltpu.SemaphoreType.DMA
    return pl.pallas_call(
        kernel,
        out_shape=(jax.ShapeDtypeStruct((TOK, WID), BF16), jax.ShapeDtypeStruct((WID, HID), F32)),
        in_specs=[vmem, vmem, vmem, hbm],
        out_specs=(vmem, hbm),
        scratch_shapes=[
            pltpu.VMEM((TOKENS, HID), BF16),
            pltpu.VMEM((TOKENS, WID), BF16),
            pltpu.VMEM((WID, HID), BF16),
            pltpu.VMEM((WID, TOKENS // 2), BF16),
            pltpu.VMEM((WID, HID), F32),
            pltpu.VMEM((NYL, TOK, WID), F32),
            pltpu.VMEM((NYH * NZ, TOK, WID), BF16),
            pltpu.VMEM((NX - 1, NYL, TOK, WID), BF16),
            pltpu.VMEM((NYL, TOK, WID), BF16),
            pltpu.VMEM((NYL - 1, TOK, WID), BF16),
            pltpu.VMEM((TOK, WID), F32),
            dma(()),
            dma((4,)),
            dma((2,)), dma((2,)),
            dma((2, 2, 5, 2)), dma((2, 2, 5, 2)),
            dma((2, 8)), dma((2, 8)),
            dma((NYL - 1,)), dma((NYL - 1,)),
            dma((NX - 1,)), dma((NX - 1,)),
            dma((NYH * NZ,)), dma((NX - 1, NYL)),
            dma((NYL,)), dma((NYL - 1,)),
        ],
        compiler_params=pltpu.CompilerParams(
            collective_id=0, has_side_effects=True, vmem_limit_bytes=48 << 20
        ),
        cost_estimate=pl.CostEstimate(
            flops=4 * TOKENS * HID * WID, bytes_accessed=8 << 20, transcendentals=ROWS * HID
        ),
    )(inputs, preact, out_grad, weight)


def solution(mesh):
    in_specs = (P("col", "row"), P("row", "col"), P("row", "col"), P("row", "col"))
    out_specs = (P("col", "row"), P("row", "col"))
    return jax.shard_map(shards, mesh=mesh, in_specs=in_specs, out_specs=out_specs, check_vma=False)
```

```python
import functools
import math

import jax
import jax.numpy as jnp
from jax import lax
from jax.experimental import pallas as pl
from jax.experimental.pallas import tpu as pltpu
from jax.sharding import PartitionSpec as P

MESH = pl.DeviceIdType.MESH
F32, BF16 = jnp.float32, jnp.bfloat16

NX, NYL, NYH, NZ = 4, 4, 2, 8
ROWS, HID, WID = 64, 1536, 384
NCH = 4
CHUNK = ROWS // NCH
PIECE = 384
TOK = 2 * ROWS
TOKENS = TOK * NYH * NZ
RIGHT, LEFT = 0, 1
PLAN = ('p00', 'f01', 'f02', 'a0', 'a1', 'a2', 'a3', 'c', 'n', 'p01', 'f03', 'p02', 'p10', 'l0', 'f11', 'x1', 'x2', 'x3', 'p03', 'p04', 'f12', 'p11', 'r00', 'r01', 'r02', 'f13', 'p12', 'p13', 'r03', 'r04', 'r10', 'l1', 'p14', 'w', 'r11', 'r12', 't0', 'o004', 'r13', 'r14', 't1', 'o104')
HALF_OF = {RIGHT: range(NCH // 2), LEFT: range(NCH // 2, NCH)}


def gelu_slope(preact_f):
    coeff = math.sqrt(2.0 / math.pi)
    inner = coeff * (preact_f + 0.044715 * preact_f * preact_f * preact_f)
    tanh_val = jnp.tanh(inner)
    return 0.5 * (1.0 + tanh_val) + 0.5 * preact_f * (1.0 - tanh_val * tanh_val) * coeff * (
        1.0 + 3.0 * 0.044715 * preact_f * preact_f
    )


def kernel(
    x_hbm, pre_hbm, grad_hbm, w_hbm, ig_ref, wg,
    pre, grad, h, xs, w, xt, g_own, g_out, g_in, s_out, s_in, g_fin,
    in_sem,
    hy_send, hy_recv, hz_send, hz_recv, hc_send, hc_recv,
    xy_send, xy_recv, xx_send, xx_recv,
    gx_send, gx_recv, gy_send, gy_recv,
):
    r, c = lax.axis_index("row"), lax.axis_index("col")
    yh, z, core = r // (2 * NZ), (r // 2) % NZ, r % 2
    x, yl = c // NYL, c % NYL

    def dev(yh_=yh, z_=z, core_=core, x_=x, yl_=yl):
        return ((yh_ * NZ + z_) * 2 + core_, x_ * NYL + yl_)

    def copy(src, dst, ssem, rsem, to):
        return pltpu.make_async_remote_copy(
            src_ref=src, dst_ref=dst, send_sem=ssem, recv_sem=rsem, device_id=to, device_id_type=MESH
        )

    def x_block(x_, yl_):
        return xs.at[pl.ds(pl.multiple_of((x_ * NYL + yl_) * TOK, TOK), TOK)]

    pre_copy = pltpu.make_async_copy(pre_hbm, pre, in_sem.at[0])
    grad_copy = pltpu.make_async_copy(grad_hbm, grad, in_sem.at[1])
    x_copy = pltpu.make_async_copy(x_hbm, x_block(x, yl), in_sem.at[2])
    w_copy = pltpu.make_async_copy(w_hbm, w, in_sem.at[3])
    for local in (pre_copy, grad_copy, x_copy, w_copy):
        local.start()

    partner = dev(yh_=1 - yh)
    sibling = dev(core_=1 - core)
    ahead, behind = dev(z_=(z + 1) % NZ), dev(z_=(z + NZ - 1) % NZ)
    peers = [partner, sibling, ahead, behind]
    peers += [dev(x_=(x + d) % NX) for d in range(1, NX)]
    peers += [dev(yl_=(yl + d) % NYL) for d in range(1, NYL)]
    barrier = pltpu.get_barrier_semaphore()
    for peer in peers:
        pl.semaphore_signal(barrier, inc=1, device_id=peer, device_id_type=MESH)

    def rows(yh_, z_, core_, chunk=None):
        base = ((yh_ * NZ + z_) * 2 + core_) * ROWS
        if chunk is None:
            return pl.ds(pl.multiple_of(base, ROWS), ROWS)
        return pl.ds(pl.multiple_of(base + chunk * CHUNK, CHUNK), CHUNK)

    def side(s):
        return yh if s == 0 else 1 - yh

    def make_hidden(chunk):
        at = pl.ds(chunk * CHUNK, CHUNK)
        h[rows(yh, z, core, chunk), :] = (
            grad[at, :].astype(F32) * gelu_slope(pre[at, :].astype(F32))
        ).astype(BF16)

    def ring(s, k, way, chunk, z_from):
        block = h.at[rows(side(s), z_from, core, chunk)]
        return copy(
            block, block, hz_send.at[s, way, k, chunk], hz_recv.at[s, way, k, chunk],
            ahead if way == RIGHT else behind,
        )

    def across(chunk, yh_):
        block = h.at[rows(yh_, z, core, chunk)]
        return copy(block, block, hy_send.at[chunk], hy_recv.at[chunk], partner)

    def share(s, slot, z_from, core_):
        block = h.at[rows(side(s), z_from, core_)]
        return copy(block, block, hc_send.at[s, slot], hc_recv.at[s, slot], sibling)

    def origin(way, k):
        return (z + NZ - k) % NZ if way == RIGHT else (z + k) % NZ

    def x_near(d, yl_):
        block = x_block(x, yl_)
        return copy(block, block, xy_send.at[d - 1], xy_recv.at[d - 1], dev(yl_=(yl + d) % NYL))

    def x_far(d, e, x_):
        block = x_block(x_, (yl + NYL - e) % NYL)
        return copy(block, block, xx_send.at[d - 1, e], xx_recv.at[d - 1, e], dev(x_=(x + d) % NX))

    def start_chunk(s, chunk):
        ring(s, 1, RIGHT, chunk, z).start()
        ring(s, 1, LEFT, chunk, z).start()

    pre_copy.wait()
    grad_copy.wait()
    make_hidden(0)
    pl.semaphore_wait(barrier, len(peers))
    for chunk in range(NCH):
        if chunk:
            make_hidden(chunk)
        across(chunk, yh).start()
        start_chunk(0, chunk)
    share(0, 0, z, core).start()
    x_copy.wait()
    for d in range(1, NX):
        x_far(d, 0, x).start()
    w_copy.wait()

    def home(s, z_from):
        return side(s) * (NZ // NYL) + z_from // NYL, z_from % NYL

    def part_out(s, z_from, x_to, j):
        d = (x + NX - x_to) % NX
        at = side(s) * NZ + z_from
        return copy(
            g_out.at[at], g_in.at[d - 1, j], gx_send.at[at], gx_recv.at[d - 1, j], dev(x_=x_to)
        )

    def product(s, slot, z_from):
        share(s, slot, z_from, 1 - core).wait_recv()
        at = pl.ds(pl.multiple_of((side(s) * NZ + z_from) * TOK, TOK), TOK)
        part = lax.dot_general(h[at, :], w[...], (((1,), (1,)), ((), ())), preferred_element_type=F32)
        x_to, j = home(s, z_from)

        @pl.when(x_to == x)
        def _():
            g_own[j] = part

        @pl.when(x_to != x)
        def _():
            g_out[side(s) * NZ + z_from] = part.astype(BF16)
            part_out(s, z_from, x_to, j).start()

    def both(fn):
        @pl.loop(0, 2)
        def _(i):
            fn(i)

    def products(s, k):
        both(lambda i: product(s, k + 3 * i, (z + NZ + (2 * i - 1) * k) % NZ))

    def sum_out(j):
        d = (yl + NYL - j) % NYL
        return copy(s_out.at[j], s_in.at[d - 1], gy_send.at[j], gy_recv.at[d - 1], dev(yl_=j))

    def reduce_x(s, z_from):
        x_to, j = home(s, z_from)

        @pl.when(x_to == x)
        def _():
            total = g_own[j]
            for d in range(1, NX):
                copy(g_out.at[0], g_in.at[d - 1, j], gx_send.at[0], gx_recv.at[d - 1, j], sibling).wait_recv()
                total = total + g_in[d - 1, j].astype(F32)

            @pl.when(j == yl)
            def _():
                g_fin[...] = total

            @pl.when(j != yl)
            def _():
                s_out[j] = total.astype(BF16)
                sum_out(j).start()

    def reduce_pair(s, k):
        both(lambda i: reduce_x(s, (z + NZ + (2 * i - 1) * k) % NZ))

    def forward(s, k):
        for chunk in range(NCH):
            for way in (RIGHT, LEFT):
                z_from = origin(way, k)
                ring(s, k, way, chunk, z_from).wait_recv()
                if k < 3 or chunk in HALF_OF[way]:
                    ring(s, k + 1, way, chunk, z_from).start()
        share(s, k, origin(RIGHT, k), core).start()
        share(s, 3 + k, origin(LEFT, k), core).start()

    def last(s):
        far = origin(RIGHT, 4)
        for i in range(NCH // 2):
            for way in (RIGHT, LEFT):
                ring(s, 4, way, HALF_OF[way][i], far).wait_recv()
        share(s, 7, far, core).start()

    half = TOKENS // 2

    def across_chunk(chunk):
        across(chunk, 1 - yh).wait_recv()
        start_chunk(1, chunk)

    def near_start():
        for d in range(1, NYL):
            x_near(d, yl).start()

    def near_pass(e):
        x_near(e, (yl + NYL - e) % NYL).wait_recv()
        for d in range(1, NX):
            x_far(d, e, x).start()

    def x_wait():
        for d in range(1, NX):
            for e in range(NYL):
                x_far(d, e, (x + NX - d) % NX).wait_recv()

    def transpose(s_):
        at = pl.multiple_of(side(s_) * half, half)
        for i in range(half // 256):
            xt[:, pl.ds(i * 256, 256)] = xs[pl.ds(at + i * 256, 256), :].T

    def outer(s_, first, n):
        at = pl.ds(pl.multiple_of(side(s_) * half, half), half)

        @pl.loop(first, first + n)
        def _(i):
            cols = pl.ds(pl.multiple_of(i * PIECE, PIECE), PIECE)
            value = jnp.dot(xt[...], h[at, cols], preferred_element_type=F32)
            if s_ == 0:
                wg[:, cols] = value
            else:
                wg[:, cols] += value

    far = origin(RIGHT, 4)
    for step in PLAN:
        what, n = step[0], [int(i) for i in step[1:]]
        if what == "f":
            forward(*n)
        elif what == "l":
            last(*n)
        elif what == "a":
            across_chunk(*n)
        elif what == "c":
            share(1, 0, z, core).start()
        elif what == "p":
            if n[1] == 0:
                product(n[0], 0, z)
            elif n[1] == 4:
                product(n[0], 7, far)
            else:
                products(*n)
        elif what == "r":
            if n[1] == 0:
                reduce_x(n[0], z)
            elif n[1] == 4:
                reduce_x(n[0], far)
            else:
                reduce_pair(*n)
        elif what == "n":
            near_start()
        elif what == "x":
            near_pass(*n)
        elif what == "w":
            x_wait()
        elif what == "t":
            transpose(*n)
        elif what == "o":
            outer(*n)

    total = g_fin[...]
    for d in range(1, NYL):
        copy(s_out.at[0], s_in.at[d - 1], gy_send.at[0], gy_recv.at[d - 1], sibling).wait_recv()
        total = total + s_in[d - 1].astype(F32)
    ig_ref[...] = total.astype(BF16)

    for chunk in range(NCH):
        across(chunk, yh).wait_send()
    for s in (0, 1):
        for way in (RIGHT, LEFT):
            for k in range(1, 5):
                for chunk in range(NCH):
                    if k < 4 or chunk in HALF_OF[way]:
                        ring(s, k, way, chunk, z).wait_send()
        for slot in range(8):
            share(s, slot, z, core).wait_send()
    for d in range(1, NYL):
        x_near(d, yl).wait_send()
    for d in range(1, NX):
        for e in range(NYL):
            x_far(d, e, x).wait_send()

    @pl.loop(0, NYH * NZ)
    def _(at):
        @pl.when(at // NYL != x)
        def _():
            copy(g_out.at[at], g_in.at[0, 0], gx_send.at[at], gx_recv.at[0, 0], sibling).wait_send()

    @pl.loop(0, NYL)
    def _(j):
        @pl.when(j != yl)
        def _():
            copy(s_out.at[j], s_in.at[0], gy_send.at[j], gy_recv.at[0], sibling).wait_send()


def shards(inputs, preact, out_grad, weight):
    vmem = pl.BlockSpec(memory_space=pltpu.VMEM)
    hbm = pl.BlockSpec(memory_space=pltpu.HBM)
    dma = pltpu.SemaphoreType.DMA
    operands = [pltpu.with_memory_space_constraint(a, pltpu.HBM) for a in (inputs, preact, out_grad, weight)]
    return pl.pallas_call(
        kernel,
        out_shape=(pltpu.VMEM((TOK, WID), BF16), pltpu.VMEM((WID, HID), F32)),
        in_specs=[hbm, hbm, hbm, hbm],
        out_specs=(vmem, vmem),
        scratch_shapes=[
            pltpu.VMEM((ROWS, HID), BF16),
            pltpu.VMEM((ROWS, HID), BF16),
            pltpu.VMEM((TOKENS, HID), BF16),
            pltpu.VMEM((TOKENS, WID), BF16),
            pltpu.VMEM((WID, HID), BF16),
            pltpu.VMEM((WID, TOKENS // 2), BF16),
            pltpu.VMEM((NYL, TOK, WID), F32),
            pltpu.VMEM((NYH * NZ, TOK, WID), BF16),
            pltpu.VMEM((NX - 1, NYL, TOK, WID), BF16),
            pltpu.VMEM((NYL, TOK, WID), BF16),
            pltpu.VMEM((NYL - 1, TOK, WID), BF16),
            pltpu.VMEM((TOK, WID), F32),
            dma((4,)),
            dma((NCH,)), dma((NCH,)),
            dma((2, 2, 5, NCH)), dma((2, 2, 5, NCH)),
            dma((2, 8)), dma((2, 8)),
            dma((NYL - 1,)), dma((NYL - 1,)),
            dma((NX - 1, NYL)), dma((NX - 1, NYL)),
            dma((NYH * NZ,)), dma((NX - 1, NYL)),
            dma((NYL,)), dma((NYL - 1,)),
        ],
        compiler_params=pltpu.CompilerParams(
            collective_id=0, has_side_effects=True, vmem_limit_bytes=48 << 20
        ),
        cost_estimate=pl.CostEstimate(
            flops=4 * TOKENS * HID * WID, bytes_accessed=8 << 20, transcendentals=ROWS * HID
        ),
    )(*operands)


def solution(mesh):
    in_specs = (P("col", "row"), P("row", "col"), P("row", "col"), P("row", "col"))
    out_specs = (P("col", "row"), P("row", "col"))
    return jax.shard_map(shards, mesh=mesh, in_specs=in_specs, out_specs=out_specs, check_vma=False)
```

```python
import functools
import math

import jax
import jax.numpy as jnp
from jax import lax
from jax.experimental import pallas as pl
from jax.experimental.pallas import tpu as pltpu
from jax.sharding import PartitionSpec as P

MESH = pl.DeviceIdType.MESH
F32, BF16 = jnp.float32, jnp.bfloat16

NX, NYL, NYH, NZ = 4, 4, 2, 8
ROWS, HID, WID = 64, 1536, 384
NCH = 2
CHUNK = ROWS // NCH
PIECE = 384
TOK = 2 * ROWS
TOKENS = TOK * NYH * NZ
RIGHT, LEFT = 0, 1
PLAN = ('p00', 'f01', 'f02', 'a0', 'a1', 'c', 'n', 'p01', 'f11', 'p02', 'p10', 'f12', 'x1', 'x2', 'x3', 'p11', 'f03', 'p12', 'p03', 'f13', 'p13', 'l0', 'p04', 'l1', 'p14', 'w', 't0', 'o004', 'r00', 'q00', 'r01', 'q01', 'r02', 'q02', 'r10', 'q10', 'r11', 'q11', 'r12', 'q12', 'r03', 'q03', 'r13', 'q13', 'r04', 'q04', 'r14', 'q14', 'd', 't1', 'o104')
SPLIT = ((0, 3), (0, 4), (1, 1), (1, 2), (1, 3), (1, 4))
HALF_OF = {RIGHT: range(NCH // 2), LEFT: range(NCH // 2, NCH)}


def gelu_slope(preact_f):
    coeff = math.sqrt(2.0 / math.pi)
    inner = coeff * (preact_f + 0.044715 * preact_f * preact_f * preact_f)
    tanh_val = jnp.tanh(inner)
    return 0.5 * (1.0 + tanh_val) + 0.5 * preact_f * (1.0 - tanh_val * tanh_val) * coeff * (
        1.0 + 3.0 * 0.044715 * preact_f * preact_f
    )


def kernel(
    x_hbm, pre_hbm, grad_hbm, w_hbm, ig_ref, wg,
    pre, grad, h, xs, w, xt, g_own, g_out, g_in, s_out, s_in, g_fin, b_own, b_in, b_out, b_far, b_fin,
    in_sem,
    hy_send, hy_recv, hz_send, hz_recv, hc_send, hc_recv,
    xy_send, xy_recv, xx_send, xx_recv,
    gx_send, gx_recv, gy_send, gy_recv, by_send, by_recv, bx_send, bx_recv,
):
    r, c = lax.axis_index("row"), lax.axis_index("col")
    yh, z, core = r // (2 * NZ), (r // 2) % NZ, r % 2
    x, yl = c // NYL, c % NYL
    split = frozenset(SPLIT)

    def dev(yh_=yh, z_=z, core_=core, x_=x, yl_=yl):
        return ((yh_ * NZ + z_) * 2 + core_, x_ * NYL + yl_)

    def copy(src, dst, ssem, rsem, to):
        return pltpu.make_async_remote_copy(
            src_ref=src, dst_ref=dst, send_sem=ssem, recv_sem=rsem, device_id=to, device_id_type=MESH
        )

    def x_block(x_, yl_):
        return xs.at[pl.ds(pl.multiple_of((x_ * NYL + yl_) * TOK, TOK), TOK)]

    pre_copy = pltpu.make_async_copy(pre_hbm, pre, in_sem.at[0])
    grad_copy = pltpu.make_async_copy(grad_hbm, grad, in_sem.at[1])
    x_copy = pltpu.make_async_copy(x_hbm, x_block(x, yl), in_sem.at[2])
    w_copy = pltpu.make_async_copy(w_hbm, w, in_sem.at[3])
    for local in (pre_copy, grad_copy, x_copy, w_copy):
        local.start()

    partner = dev(yh_=1 - yh)
    sibling = dev(core_=1 - core)
    ahead, behind = dev(z_=(z + 1) % NZ), dev(z_=(z + NZ - 1) % NZ)
    peers = [partner, sibling, ahead, behind]
    peers += [dev(x_=(x + d) % NX) for d in range(1, NX)]
    peers += [dev(yl_=(yl + d) % NYL) for d in range(1, NYL)]
    barrier = pltpu.get_barrier_semaphore()
    for peer in peers:
        pl.semaphore_signal(barrier, inc=1, device_id=peer, device_id_type=MESH)

    def rows(yh_, z_, core_, chunk=None):
        base = ((yh_ * NZ + z_) * 2 + core_) * ROWS
        if chunk is None:
            return pl.ds(pl.multiple_of(base, ROWS), ROWS)
        return pl.ds(pl.multiple_of(base + chunk * CHUNK, CHUNK), CHUNK)

    def side(s):
        return yh if s == 0 else 1 - yh

    def make_hidden(chunk):
        at = pl.ds(chunk * CHUNK, CHUNK)
        h[rows(yh, z, core, chunk), :] = (
            grad[at, :].astype(F32) * gelu_slope(pre[at, :].astype(F32))
        ).astype(BF16)

    def ring(s, k, way, chunk, z_from):
        block = h.at[rows(side(s), z_from, core, chunk)]
        return copy(
            block, block, hz_send.at[s, way, k, chunk], hz_recv.at[s, way, k, chunk],
            ahead if way == RIGHT else behind,
        )

    def across(chunk, yh_):
        block = h.at[rows(yh_, z, core, chunk)]
        return copy(block, block, hy_send.at[chunk], hy_recv.at[chunk], partner)

    def share(s, slot, z_from, core_):
        block = h.at[rows(side(s), z_from, core_)]
        return copy(block, block, hc_send.at[s, slot], hc_recv.at[s, slot], sibling)

    def origin(way, k):
        return (z + NZ - k) % NZ if way == RIGHT else (z + k) % NZ

    def x_near(d, yl_):
        block = x_block(x, yl_)
        return copy(block, block, xy_send.at[d - 1], xy_recv.at[d - 1], dev(yl_=(yl + d) % NYL))

    def x_far(d, e, x_):
        block = x_block(x_, (yl + NYL - e) % NYL)
        return copy(block, block, xx_send.at[d - 1, e], xx_recv.at[d - 1, e], dev(x_=(x + d) % NX))

    def start_chunk(s, chunk):
        ring(s, 1, RIGHT, chunk, z).start()
        ring(s, 1, LEFT, chunk, z).start()

    pre_copy.wait()
    grad_copy.wait()
    make_hidden(0)
    pl.semaphore_wait(barrier, len(peers))
    for chunk in range(NCH):
        if chunk:
            make_hidden(chunk)
        across(chunk, yh).start()
        start_chunk(0, chunk)
    share(0, 0, z, core).start()
    x_copy.wait()
    for d in range(1, NX):
        x_far(d, 0, x).start()
    w_copy.wait()

    def home(s, z_from):
        return side(s) * (NZ // NYL) + z_from // NYL, z_from % NYL

    def top(s, k):
        return pl.ds(0, ROWS if (s, k) in split else TOK)

    low = pl.ds(ROWS, ROWS)

    def part_out(s, k, z_from, x_to, j):
        d = (x + NX - x_to) % NX
        at = side(s) * NZ + z_from
        return copy(
            g_out.at[at, top(s, k)], g_in.at[d - 1, j, top(s, k)], gx_send.at[at], gx_recv.at[d - 1, j],
            dev(x_=x_to),
        )

    def low_out(s, z_from, x_to, j):
        d = (yl + NYL - j) % NYL
        at = side(s) * NZ + z_from
        return copy(g_out.at[at, low], b_in.at[d - 1, x_to], by_send.at[at], by_recv.at[d - 1, x_to], dev(yl_=j))

    def product(s, k, slot, z_from):
        share(s, slot, z_from, 1 - core).wait_recv()
        at = side(s) * NZ + z_from
        rows_at = pl.ds(pl.multiple_of(at * TOK, TOK), TOK)
        part = lax.dot_general(h[rows_at, :], w[...], (((1,), (1,)), ((), ())), preferred_element_type=F32)
        x_to, j = home(s, z_from)
        g_out[at] = part.astype(BF16)

        @pl.when(x_to == x)
        def _():
            g_own[j] = part

        @pl.when(x_to != x)
        def _():
            part_out(s, k, z_from, x_to, j).start()

        if (s, k) in split:
            @pl.when(j == yl)
            def _():
                b_own[x_to] = part[ROWS:, :]

            @pl.when(j != yl)
            def _():
                low_out(s, z_from, x_to, j).start()

    def each(k, fn):
        if k == 0:
            fn(0, z)
        elif k == 4:
            fn(7, origin(RIGHT, 4))
        else:
            @pl.loop(0, 2)
            def _(i):
                fn(k + 3 * i, (z + NZ + (2 * i - 1) * k) % NZ)

    def products(s, k):
        each(k, lambda slot, z_from: product(s, k, slot, z_from))

    def sum_out(s, k, j):
        d = (yl + NYL - j) % NYL
        return copy(
            s_out.at[j, top(s, k)], s_in.at[d - 1, top(s, k)], gy_send.at[j], gy_recv.at[d - 1], dev(yl_=j)
        )

    def low_sum(x_to):
        d = (x + NX - x_to) % NX
        return copy(b_out.at[x_to], b_far.at[d - 1], bx_send.at[x_to], bx_recv.at[d - 1], dev(x_=x_to))

    def reduce_x(s, k):
        rows_ = top(s, k)

        def one(slot, z_from):
            x_to, j = home(s, z_from)

            @pl.when(x_to == x)
            def _():
                total = g_own[j, rows_]
                for d in range(1, NX):
                    here = g_in.at[d - 1, j, rows_]
                    copy(here, here, gx_send.at[0], gx_recv.at[d - 1, j], sibling).wait_recv()
                    total = total + here[...].astype(F32)

                @pl.when(j == yl)
                def _():
                    g_fin[rows_] = total

                @pl.when(j != yl)
                def _():
                    s_out[j, rows_] = total.astype(BF16)
                    sum_out(s, k, j).start()

        each(k, one)

    def reduce_y(s, k):
        def one(slot, z_from):
            x_to, j = home(s, z_from)

            @pl.when(j == yl)
            def _():
                total = b_own[x_to]
                for d in range(1, NYL):
                    here = b_in.at[d - 1, x_to]
                    copy(here, here, by_send.at[0], by_recv.at[d - 1, x_to], sibling).wait_recv()
                    total = total + here[...].astype(F32)

                @pl.when(x_to == x)
                def _():
                    b_fin[...] = total

                @pl.when(x_to != x)
                def _():
                    b_out[x_to] = total.astype(BF16)
                    low_sum(x_to).start()

        if (s, k) in split:
            each(k, one)

    def forward(s, k):
        for chunk in range(NCH):
            for way in (RIGHT, LEFT):
                z_from = origin(way, k)
                ring(s, k, way, chunk, z_from).wait_recv()
                if k < 3 or chunk in HALF_OF[way]:
                    ring(s, k + 1, way, chunk, z_from).start()
        share(s, k, origin(RIGHT, k), core).start()
        share(s, 3 + k, origin(LEFT, k), core).start()

    def last(s):
        far = origin(RIGHT, 4)
        for i in range(NCH // 2):
            for way in (RIGHT, LEFT):
                ring(s, 4, way, HALF_OF[way][i], far).wait_recv()
        share(s, 7, far, core).start()

    half = TOKENS // 2

    def across_chunk(chunk):
        across(chunk, 1 - yh).wait_recv()
        start_chunk(1, chunk)

    def near_start():
        for d in range(1, NYL):
            x_near(d, yl).start()

    def near_pass(e):
        x_near(e, (yl + NYL - e) % NYL).wait_recv()
        for d in range(1, NX):
            x_far(d, e, x).start()

    def x_wait():
        for d in range(1, NX):
            for e in range(NYL):
                x_far(d, e, (x + NX - d) % NX).wait_recv()

    def transpose(s_):
        at = pl.multiple_of(side(s_) * half, half)
        for i in range(half // 256):
            xt[:, pl.ds(i * 256, 256)] = xs[pl.ds(at + i * 256, 256), :].T

    def outer(s_, first, n):
        at = pl.ds(pl.multiple_of(side(s_) * half, half), half)

        @pl.loop(first, first + n)
        def _(i):
            cols = pl.ds(pl.multiple_of(i * PIECE, PIECE), PIECE)
            value = jnp.dot(xt[...], h[at, cols], preferred_element_type=F32)
            if s_ == 0:
                wg[:, cols] = value
            else:
                wg[:, cols] += value

    def drain():
        for chunk in range(NCH):
            across(chunk, yh).wait_send()
        for s in (0, 1):
            for way in (RIGHT, LEFT):
                for k in range(1, 5):
                    for chunk in range(NCH):
                        if k < 4 or chunk in HALF_OF[way]:
                            ring(s, k, way, chunk, z).wait_send()
            for slot in range(8):
                share(s, slot, z, core).wait_send()
        for d in range(1, NYL):
            x_near(d, yl).wait_send()
        for d in range(1, NX):
            for e in range(NYL):
                x_far(d, e, x).wait_send()

    def sent(s, k):
        def one(slot, z_from):
            x_to, j = home(s, z_from)

            @pl.when(x_to != x)
            def _():
                part_out(s, k, z_from, x_to, j).wait_send()

            @pl.when((x_to == x) & (j != yl))
            def _():
                sum_out(s, k, j).wait_send()

            if (s, k) in split:
                @pl.when(j != yl)
                def _():
                    low_out(s, z_from, x_to, j).wait_send()

                @pl.when((j == yl) & (x_to != x))
                def _():
                    low_sum(x_to).wait_send()

        each(k, one)

    for step in PLAN:
        what, n = step[0], [int(i) for i in step[1:]]
        if what == "f":
            forward(*n)
        elif what == "l":
            last(*n)
        elif what == "a":
            across_chunk(*n)
        elif what == "c":
            share(1, 0, z, core).start()
        elif what == "p":
            products(*n)
        elif what == "r":
            reduce_x(*n)
        elif what == "q":
            reduce_y(*n)
        elif what == "n":
            near_start()
        elif what == "x":
            near_pass(*n)
        elif what == "w":
            x_wait()
        elif what == "t":
            transpose(*n)
        elif what == "o":
            outer(*n)
        elif what == "d":
            drain()

    def finish(rows_, first, arrived, recv):
        total = first
        for d in range(1, NYL):
            here = arrived.at[d - 1, rows_]
            copy(here, here, gy_send.at[0], recv.at[d - 1], sibling).wait_recv()
            total = total + here[...].astype(F32)
        return total.astype(BF16)

    def final(s, k):
        def one(slot, z_from):
            x_to, j = home(s, z_from)

            @pl.when((x_to == x) & (j == yl))
            def _():
                rows_ = top(s, k)
                ig_ref[rows_, :] = finish(rows_, g_fin[rows_], s_in, gy_recv)
                if (s, k) in split:
                    all_ = pl.ds(0, ROWS)
                    ig_ref[low, :] = finish(all_, b_fin[...], b_far, bx_recv)

        each(k, one)

    for s in (0, 1):
        for k in range(5):
            sent(s, k)
    for s in (0, 1):
        for k in range(5):
            final(s, k)


def shards(inputs, preact, out_grad, weight):
    vmem = pl.BlockSpec(memory_space=pltpu.VMEM)
    hbm = pl.BlockSpec(memory_space=pltpu.HBM)
    dma = pltpu.SemaphoreType.DMA
    operands = [pltpu.with_memory_space_constraint(a, pltpu.HBM) for a in (inputs, preact, out_grad, weight)]
    return pl.pallas_call(
        kernel,
        out_shape=(pltpu.VMEM((TOK, WID), BF16), pltpu.VMEM((WID, HID), F32)),
        in_specs=[hbm, hbm, hbm, hbm],
        out_specs=(vmem, vmem),
        scratch_shapes=[
            pltpu.VMEM((ROWS, HID), BF16),
            pltpu.VMEM((ROWS, HID), BF16),
            pltpu.VMEM((TOKENS, HID), BF16),
            pltpu.VMEM((TOKENS, WID), BF16),
            pltpu.VMEM((WID, HID), BF16),
            pltpu.VMEM((WID, TOKENS // 2), BF16),
            pltpu.VMEM((NYL, TOK, WID), F32),
            pltpu.VMEM((NYH * NZ, TOK, WID), BF16),
            pltpu.VMEM((NX - 1, NYL, TOK, WID), BF16),
            pltpu.VMEM((NYL, TOK, WID), BF16),
            pltpu.VMEM((NYL - 1, TOK, WID), BF16),
            pltpu.VMEM((TOK, WID), F32),
            pltpu.VMEM((NX, ROWS, WID), F32),
            pltpu.VMEM((NYL - 1, NX, ROWS, WID), BF16),
            pltpu.VMEM((NX, ROWS, WID), BF16),
            pltpu.VMEM((NX - 1, ROWS, WID), BF16),
            pltpu.VMEM((ROWS, WID), F32),
            dma((4,)),
            dma((NCH,)), dma((NCH,)),
            dma((2, 2, 5, NCH)), dma((2, 2, 5, NCH)),
            dma((2, 8)), dma((2, 8)),
            dma((NYL - 1,)), dma((NYL - 1,)),
            dma((NX - 1, NYL)), dma((NX - 1, NYL)),
            dma((NYH * NZ,)), dma((NX - 1, NYL)),
            dma((NYL,)), dma((NYL - 1,)),
            dma((NYH * NZ,)), dma((NYL - 1, NX)),
            dma((NX,)), dma((NX - 1,)),
        ],
        compiler_params=pltpu.CompilerParams(
            collective_id=0, has_side_effects=True, vmem_limit_bytes=48 << 20
        ),
        cost_estimate=pl.CostEstimate(
            flops=4 * TOKENS * HID * WID, bytes_accessed=8 << 20, transcendentals=ROWS * HID
        ),
    )(*operands)


def solution(mesh):
    in_specs = (P("col", "row"), P("row", "col"), P("row", "col"), P("row", "col"))
    out_specs = (P("col", "row"), P("row", "col"))
    return jax.shard_map(shards, mesh=mesh, in_specs=in_specs, out_specs=out_specs, check_vma=False)
```

```python
import functools
import math

import jax
import jax.numpy as jnp
from jax import lax
from jax.experimental import pallas as pl
from jax.experimental.pallas import tpu as pltpu
from jax.sharding import PartitionSpec as P

MESH = pl.DeviceIdType.MESH
F32, BF16 = jnp.float32, jnp.bfloat16

NX, NYL, NYH, NZ = 4, 4, 2, 8
ROWS, HID, WID = 64, 1536, 384
NCH = 2
CHUNK = ROWS // NCH
PIECE = 384
TOK = 2 * ROWS
TOKENS = TOK * NYH * NZ
RIGHT, LEFT = 0, 1
PLAN = (
    "p00", "f01", "f02", "a0", "a1", "c", "n", "p01", "f11", "p02", "p10", "x1", "x2", "x3", "f12", "p11",
    "f03", "p12", "p03", "f13", "p13", "l0", "p04", "l1", "p14", "w", "t0", "o004", "r00", "q00", "r01",
    "q01", "r02", "q02", "r10", "q10", "r11", "q11", "r12", "q12", "r03", "q03", "r13", "q13", "r04", "q04",
    "r14", "q14", "d", "t1", "o104",
)
SPLIT = tuple((s, k) for s in (0, 1) for k in range(5))
HALF_OF = {RIGHT: range(NCH // 2), LEFT: range(NCH // 2, NCH)}


def gelu_slope(preact_f):
    coeff = math.sqrt(2.0 / math.pi)
    inner = coeff * (preact_f + 0.044715 * preact_f * preact_f * preact_f)
    tanh_val = jnp.tanh(inner)
    return 0.5 * (1.0 + tanh_val) + 0.5 * preact_f * (1.0 - tanh_val * tanh_val) * coeff * (
        1.0 + 3.0 * 0.044715 * preact_f * preact_f
    )


def kernel(
    x_hbm, pre_hbm, grad_hbm, w_hbm, ig_ref, wg,
    pre, grad, h, xs, w, wt, xt, g_own, g_out, g_in, s_out, s_in, g_fin, b_own, b_in, b_out, b_far, b_fin,
    in_sem,
    hy_send, hy_recv, hz_send, hz_recv, hc_send, hc_recv,
    xy_send, xy_recv, xx_send, xx_recv,
    gx_send, gx_recv, gy_send, gy_recv, by_send, by_recv, bx_send, bx_recv,
):
    r, c = lax.axis_index("row"), lax.axis_index("col")
    yh, z, core = r // (2 * NZ), (r // 2) % NZ, r % 2
    x, yl = c // NYL, c % NYL
    split = frozenset(SPLIT)

    def dev(yh_=yh, z_=z, core_=core, x_=x, yl_=yl):
        return ((yh_ * NZ + z_) * 2 + core_, x_ * NYL + yl_)

    def copy(src, dst, ssem, rsem, to):
        return pltpu.make_async_remote_copy(
            src_ref=src, dst_ref=dst, send_sem=ssem, recv_sem=rsem, device_id=to, device_id_type=MESH
        )

    def x_block(x_, yl_):
        return xs.at[pl.ds(pl.multiple_of((x_ * NYL + yl_) * TOK, TOK), TOK)]

    pre_copy = pltpu.make_async_copy(pre_hbm, pre, in_sem.at[0])
    grad_copy = pltpu.make_async_copy(grad_hbm, grad, in_sem.at[1])
    x_copy = pltpu.make_async_copy(x_hbm, x_block(x, yl), in_sem.at[2])
    w_copy = pltpu.make_async_copy(w_hbm, w, in_sem.at[3])
    for local in (pre_copy, grad_copy, x_copy, w_copy):
        local.start()

    partner = dev(yh_=1 - yh)
    sibling = dev(core_=1 - core)
    ahead, behind = dev(z_=(z + 1) % NZ), dev(z_=(z + NZ - 1) % NZ)
    peers = [partner, sibling, ahead, behind]
    peers += [dev(x_=(x + d) % NX) for d in range(1, NX)]
    peers += [dev(yl_=(yl + d) % NYL) for d in range(1, NYL)]
    barrier = pltpu.get_barrier_semaphore()
    for peer in peers:
        pl.semaphore_signal(barrier, inc=1, device_id=peer, device_id_type=MESH)

    def rows(yh_, z_, core_, chunk=None):
        base = ((yh_ * NZ + z_) * 2 + core_) * ROWS
        if chunk is None:
            return pl.ds(pl.multiple_of(base, ROWS), ROWS)
        return pl.ds(pl.multiple_of(base + chunk * CHUNK, CHUNK), CHUNK)

    def side(s):
        return yh if s == 0 else 1 - yh

    def make_hidden(chunk):
        at = pl.ds(chunk * CHUNK, CHUNK)
        h[rows(yh, z, core, chunk), :] = (
            grad[at, :].astype(F32) * gelu_slope(pre[at, :].astype(F32))
        ).astype(BF16)

    def ring(s, k, way, chunk, z_from):
        block = h.at[rows(side(s), z_from, core, chunk)]
        return copy(
            block, block, hz_send.at[s, way, k, chunk], hz_recv.at[s, way, k, chunk],
            ahead if way == RIGHT else behind,
        )

    def across(chunk, yh_):
        block = h.at[rows(yh_, z, core, chunk)]
        return copy(block, block, hy_send.at[chunk], hy_recv.at[chunk], partner)

    def share(s, slot, z_from, core_):
        block = h.at[rows(side(s), z_from, core_)]
        return copy(block, block, hc_send.at[s, slot], hc_recv.at[s, slot], sibling)

    def origin(way, k):
        return (z + NZ - k) % NZ if way == RIGHT else (z + k) % NZ

    def x_near(d, yl_):
        block = x_block(x, yl_)
        return copy(block, block, xy_send.at[d - 1], xy_recv.at[d - 1], dev(yl_=(yl + d) % NYL))

    def x_far(d, e, x_):
        block = x_block(x_, (yl + NYL - e) % NYL)
        return copy(block, block, xx_send.at[d - 1, e], xx_recv.at[d - 1, e], dev(x_=(x + d) % NX))

    def start_chunk(s, chunk):
        ring(s, 1, RIGHT, chunk, z).start()
        ring(s, 1, LEFT, chunk, z).start()

    pre_copy.wait()
    grad_copy.wait()
    make_hidden(0)
    pl.semaphore_wait(barrier, len(peers))
    for chunk in range(NCH):
        if chunk:
            make_hidden(chunk)
        across(chunk, yh).start()
        start_chunk(0, chunk)
    share(0, 0, z, core).start()
    x_copy.wait()
    for d in range(1, NX):
        x_far(d, 0, x).start()
    w_copy.wait()
    for i in range(HID // 256):
        at = pl.ds(i * 256, 256)
        wt[at, :] = w[:, at].T

    def home(s, z_from):
        return side(s) * (NZ // NYL) + z_from // NYL, z_from % NYL

    def top(s, k):
        return pl.ds(0, ROWS if (s, k) in split else TOK)

    low = pl.ds(ROWS, ROWS)

    def part_out(s, k, z_from, x_to, j):
        d = (x + NX - x_to) % NX
        at = side(s) * NZ + z_from
        return copy(
            g_out.at[at, top(s, k)], g_in.at[d - 1, j, top(s, k)], gx_send.at[at], gx_recv.at[d - 1, j],
            dev(x_=x_to),
        )

    def low_out(s, z_from, x_to, j):
        d = (yl + NYL - j) % NYL
        at = side(s) * NZ + z_from
        return copy(g_out.at[at, low], b_in.at[d - 1, x_to], by_send.at[at], by_recv.at[d - 1, x_to], dev(yl_=j))

    def product(s, k, slot, z_from):
        share(s, slot, z_from, 1 - core).wait_recv()
        at = side(s) * NZ + z_from
        rows_at = pl.ds(pl.multiple_of(at * TOK, TOK), TOK)
        part = jnp.dot(h[rows_at, :], wt[...], preferred_element_type=F32)
        x_to, j = home(s, z_from)
        g_out[at] = part.astype(BF16)

        @pl.when(x_to == x)
        def _():
            g_own[j] = part

        @pl.when(x_to != x)
        def _():
            part_out(s, k, z_from, x_to, j).start()

        if (s, k) in split:
            @pl.when(j == yl)
            def _():
                b_own[x_to] = part[ROWS:, :]

            @pl.when(j != yl)
            def _():
                low_out(s, z_from, x_to, j).start()

    def each(k, fn):
        if k == 0:
            fn(0, z)
        elif k == 4:
            fn(7, origin(RIGHT, 4))
        else:
            @pl.loop(0, 2)
            def _(i):
                fn(k + 3 * i, (z + NZ + (2 * i - 1) * k) % NZ)

    def products(s, k):
        each(k, lambda slot, z_from: product(s, k, slot, z_from))

    def sum_out(s, k, j):
        d = (yl + NYL - j) % NYL
        return copy(
            s_out.at[j, top(s, k)], s_in.at[d - 1, top(s, k)], gy_send.at[j], gy_recv.at[d - 1], dev(yl_=j)
        )

    def low_sum(x_to):
        d = (x + NX - x_to) % NX
        return copy(b_out.at[x_to], b_far.at[d - 1], bx_send.at[x_to], bx_recv.at[d - 1], dev(x_=x_to))

    def reduce_x(s, k):
        rows_ = top(s, k)

        def one(slot, z_from):
            x_to, j = home(s, z_from)

            @pl.when(x_to == x)
            def _():
                total = g_own[j, rows_]
                for d in range(1, NX):
                    here = g_in.at[d - 1, j, rows_]
                    copy(here, here, gx_send.at[0], gx_recv.at[d - 1, j], sibling).wait_recv()
                    total = total + here[...].astype(F32)

                @pl.when(j == yl)
                def _():
                    g_fin[rows_] = total

                @pl.when(j != yl)
                def _():
                    s_out[j, rows_] = total.astype(BF16)
                    sum_out(s, k, j).start()

        each(k, one)

    def reduce_y(s, k):
        def one(slot, z_from):
            x_to, j = home(s, z_from)

            @pl.when(j == yl)
            def _():
                total = b_own[x_to]
                for d in range(1, NYL):
                    here = b_in.at[d - 1, x_to]
                    copy(here, here, by_send.at[0], by_recv.at[d - 1, x_to], sibling).wait_recv()
                    total = total + here[...].astype(F32)

                @pl.when(x_to == x)
                def _():
                    b_fin[...] = total

                @pl.when(x_to != x)
                def _():
                    b_out[x_to] = total.astype(BF16)
                    low_sum(x_to).start()

        if (s, k) in split:
            each(k, one)

    def forward(s, k):
        for chunk in range(NCH):
            for way in (RIGHT, LEFT):
                z_from = origin(way, k)
                ring(s, k, way, chunk, z_from).wait_recv()
                if k < 3 or chunk in HALF_OF[way]:
                    ring(s, k + 1, way, chunk, z_from).start()
        share(s, k, origin(RIGHT, k), core).start()
        share(s, 3 + k, origin(LEFT, k), core).start()

    def last(s):
        far = origin(RIGHT, 4)
        for i in range(NCH // 2):
            for way in (RIGHT, LEFT):
                ring(s, 4, way, HALF_OF[way][i], far).wait_recv()
        share(s, 7, far, core).start()

    half = TOKENS // 2

    def across_chunk(chunk):
        across(chunk, 1 - yh).wait_recv()
        start_chunk(1, chunk)

    def near_start():
        for d in range(1, NYL):
            x_near(d, yl).start()

    def near_pass(e):
        x_near(e, (yl + NYL - e) % NYL).wait_recv()
        for d in range(1, NX):
            x_far(d, e, x).start()

    def x_wait():
        for d in range(1, NX):
            for e in range(NYL):
                x_far(d, e, (x + NX - d) % NX).wait_recv()

    def transpose(s_):
        at = pl.multiple_of(side(s_) * half, half)
        for i in range(half // 256):
            xt[:, pl.ds(i * 256, 256)] = xs[pl.ds(at + i * 256, 256), :].T

    def outer(s_, first, n):
        at = pl.ds(pl.multiple_of(side(s_) * half, half), half)

        @pl.loop(first, first + n)
        def _(i):
            cols = pl.ds(pl.multiple_of(i * PIECE, PIECE), PIECE)
            value = jnp.dot(xt[...], h[at, cols], preferred_element_type=F32)
            if s_ == 0:
                wg[:, cols] = value
            else:
                wg[:, cols] += value

    def drain():
        for chunk in range(NCH):
            across(chunk, yh).wait_send()
        for s in (0, 1):
            for way in (RIGHT, LEFT):
                for k in range(1, 5):
                    for chunk in range(NCH):
                        if k < 4 or chunk in HALF_OF[way]:
                            ring(s, k, way, chunk, z).wait_send()
            for slot in range(8):
                share(s, slot, z, core).wait_send()
        for d in range(1, NYL):
            x_near(d, yl).wait_send()
        for d in range(1, NX):
            for e in range(NYL):
                x_far(d, e, x).wait_send()

    def sent(s, k):
        def one(slot, z_from):
            x_to, j = home(s, z_from)

            @pl.when(x_to != x)
            def _():
                part_out(s, k, z_from, x_to, j).wait_send()

            @pl.when((x_to == x) & (j != yl))
            def _():
                sum_out(s, k, j).wait_send()

            if (s, k) in split:
                @pl.when(j != yl)
                def _():
                    low_out(s, z_from, x_to, j).wait_send()

                @pl.when((j == yl) & (x_to != x))
                def _():
                    low_sum(x_to).wait_send()

        each(k, one)

    for step in PLAN:
        what, n = step[0], [int(i) for i in step[1:]]
        if what == "f":
            forward(*n)
        elif what == "l":
            last(*n)
        elif what == "a":
            across_chunk(*n)
        elif what == "c":
            share(1, 0, z, core).start()
        elif what == "p":
            products(*n)
        elif what == "r":
            reduce_x(*n)
        elif what == "q":
            reduce_y(*n)
        elif what == "n":
            near_start()
        elif what == "x":
            near_pass(*n)
        elif what == "w":
            x_wait()
        elif what == "t":
            transpose(*n)
        elif what == "o":
            outer(*n)
        elif what == "d":
            drain()

    def finish(rows_, first, arrived, recv):
        total = first
        for d in range(1, NYL):
            here = arrived.at[d - 1, rows_]
            copy(here, here, gy_send.at[0], recv.at[d - 1], sibling).wait_recv()
            total = total + here[...].astype(F32)
        return total.astype(BF16)

    def final(s, k):
        def one(slot, z_from):
            x_to, j = home(s, z_from)

            @pl.when((x_to == x) & (j == yl))
            def _():
                rows_ = top(s, k)
                ig_ref[rows_, :] = finish(rows_, g_fin[rows_], s_in, gy_recv)
                if (s, k) in split:
                    all_ = pl.ds(0, ROWS)
                    ig_ref[low, :] = finish(all_, b_fin[...], b_far, bx_recv)

        each(k, one)

    for s in (0, 1):
        for k in range(5):
            sent(s, k)
    for s in (0, 1):
        for k in range(5):
            final(s, k)


def shards(inputs, preact, out_grad, weight):
    vmem = pl.BlockSpec(memory_space=pltpu.VMEM)
    hbm = pl.BlockSpec(memory_space=pltpu.HBM)
    dma = pltpu.SemaphoreType.DMA
    operands = [pltpu.with_memory_space_constraint(a, pltpu.HBM) for a in (inputs, preact, out_grad, weight)]
    return pl.pallas_call(
        kernel,
        out_shape=(pltpu.VMEM((TOK, WID), BF16), pltpu.VMEM((WID, HID), F32)),
        in_specs=[hbm, hbm, hbm, hbm],
        out_specs=(vmem, vmem),
        scratch_shapes=[
            pltpu.VMEM((ROWS, HID), BF16),
            pltpu.VMEM((ROWS, HID), BF16),
            pltpu.VMEM((TOKENS, HID), BF16),
            pltpu.VMEM((TOKENS, WID), BF16),
            pltpu.VMEM((WID, HID), BF16),
            pltpu.VMEM((HID, WID), BF16),
            pltpu.VMEM((WID, TOKENS // 2), BF16),
            pltpu.VMEM((NYL, TOK, WID), F32),
            pltpu.VMEM((NYH * NZ, TOK, WID), BF16),
            pltpu.VMEM((NX - 1, NYL, TOK, WID), BF16),
            pltpu.VMEM((NYL, TOK, WID), BF16),
            pltpu.VMEM((NYL - 1, TOK, WID), BF16),
            pltpu.VMEM((TOK, WID), F32),
            pltpu.VMEM((NX, ROWS, WID), F32),
            pltpu.VMEM((NYL - 1, NX, ROWS, WID), BF16),
            pltpu.VMEM((NX, ROWS, WID), BF16),
            pltpu.VMEM((NX - 1, ROWS, WID), BF16),
            pltpu.VMEM((ROWS, WID), F32),
            dma((4,)),
            dma((NCH,)), dma((NCH,)),
            dma((2, 2, 5, NCH)), dma((2, 2, 5, NCH)),
            dma((2, 8)), dma((2, 8)),
            dma((NYL - 1,)), dma((NYL - 1,)),
            dma((NX - 1, NYL)), dma((NX - 1, NYL)),
            dma((NYH * NZ,)), dma((NX - 1, NYL)),
            dma((NYL,)), dma((NYL - 1,)),
            dma((NYH * NZ,)), dma((NYL - 1, NX)),
            dma((NX,)), dma((NX - 1,)),
        ],
        compiler_params=pltpu.CompilerParams(
            collective_id=0, has_side_effects=True, vmem_limit_bytes=48 << 20
        ),
        cost_estimate=pl.CostEstimate(
            flops=4 * TOKENS * HID * WID, bytes_accessed=8 << 20, transcendentals=ROWS * HID
        ),
    )(*operands)


def solution(mesh):
    in_specs = (P("col", "row"), P("row", "col"), P("row", "col"), P("row", "col"))
    out_specs = (P("col", "row"), P("row", "col"))
    return jax.shard_map(shards, mesh=mesh, in_specs=in_specs, out_specs=out_specs, check_vma=False)
```
